128 devices in a mesh: row: 4 (over y_hi, core), col: 32 (over z, y_lo, x).
Axes of the slice: x: 4, y: 4 (y_hi: 2, y_lo: 2; y = y_hi * 2 + y_lo), z: 4, core: 2. Of those that a mesh axis runs over, the one named last changes fastest.
Arguments:
- pair_amps: float32 [640, 25600], P('row', 'col'), may hold values from -6 to 6
- cycle_w: float32 [25600, 25600], P('row', 'col'), may hold values from -0.0390625 to 0.0390625
Outputs:
- cycle_term: float32 [640, 25600], P('row', 'col')
The draws below stay inside these ranges and needn't reach their ends.
All inputs are finite; a program needn't handle non-finite values.
Results may differ from the reference program's by a relative error of at most 0.00007.
Values sent between devices are 32-bit elements; how exact they have to be, the bound alone decides.
No kernel may reach another device: no remote copies, remote signals or barrier semaphores. Data moves between devices by JAX's collectives and lax.ppermute only.
A program may use at most 192 MiB of HBM per device.

```python
import jax
import jax.numpy as jnp
from jax import lax

O = 40
V = 640
A_SLAB = 16
OV = 25600
PAIRS = 1600


def block_levels(own_key, shape, pieces, smallest, high):
    level, own = 1.0, jax.random.fold_in(own_key, 6)
    for axis_at, parts in pieces:
        draws = jnp.exp(jax.random.uniform(jax.random.fold_in(own, axis_at), (parts,), jnp.float32, smallest / len(pieces), high / len(pieces)))
        level = level * jnp.repeat(draws, shape[axis_at] // parts).reshape([-1 if axis == axis_at else 1 for axis in range(len(shape))])
    return level


def scatter_about(stream_key, extent, spread, limit, pieces=(), kind=jnp.bfloat16):
    result = jax.random.normal(stream_key, extent, jnp.float32) * spread
    if len(pieces) > 0:
        result = block_levels(stream_key, extent, pieces, -0.22, 0.18) * result
    return jnp.clip(result, min=-limit, max=limit).astype(kind)


def setup_inputs(seed: int = 0) -> dict:
    arg_keys = jax.random.split(jax.random.key(seed), 3)
    return {
        "pair_amps": scatter_about(arg_keys[0], (V, PAIRS * A_SLAB), 1.0, 6.0, ((0, 4), (1, 32)), jnp.float32),
        "cycle_w": scatter_about(arg_keys[1], (OV, OV), OV ** -0.5, 0.0390625, ((0, 4), (1, 32)), jnp.float32),
    }


def reference(pair_amps, cycle_w):
    amp_panel = pair_amps.reshape(V, O, O, A_SLAB).transpose(3, 1, 0, 2).reshape(A_SLAB * O, V * O)
    return jnp.dot(amp_panel, cycle_w, precision=lax.Precision.HIGHEST, preferred_element_type=jnp.float32)
```

```python
import functools

import jax
import jax.numpy as jnp
from jax import lax
from jax.experimental import pallas as pl
from jax.experimental.pallas import tpu as pltpu
from jax.sharding import PartitionSpec as P

O = 40
PAY = 63
KMAIN, KTAIL = 5120, 1280
KBLK = 1280
VLIM = 56 * 1024 * 1024


def pack_kernel(sc_ref, p_ref, o0_ref, o1_ref, main, tail):
    base = pl.multiple_of(sc_ref[0] * 32, 32)
    tail[...] = jnp.zeros_like(tail)
    for k in range(7):
        if k < 6:
            x = p_ref[:, 128 * k : 128 * k + 128]
            rows = 128
        else:
            x = jnp.concatenate([p_ref[:, 768:800], jnp.zeros((160, 96), jnp.float32)], axis=1)
            rows = 32
        x = jnp.concatenate([x, jnp.zeros((96, 128), jnp.float32)], axis=0)
        xt = x.T
        main[128 * k : 128 * k + rows, :] = xt[:rows, :128]
        tail[pl.ds(base + 128 * k, rows), :] = xt[:rows, 128:]
    for h, o_ref in ((0, o0_ref), (1, o1_ref)):
        for s in range(8):
            a = 4 * (s // 2) + 2 * h + s % 2
            o_ref[pl.ds(s, 50, stride=8), :] = main[pl.ds(a, 50, stride=16), :]
            t = tail[pl.ds(a, 13, stride=64), :]
            for q in range(1, 4):
                t = t + pltpu.roll(tail[pl.ds(16 * q + a, 13, stride=64), :], 32 * q, 1)
            o_ref[pl.ds(400 + s, 13, stride=8), :] = t


def pack(scal, p):
    full = pl.BlockSpec(memory_space=pltpu.VMEM)
    return pl.pallas_call(
        pack_kernel,
        out_shape=[jax.ShapeDtypeStruct((PAY * 8, 128), jnp.float32)] * 2,
        in_specs=[pl.BlockSpec(memory_space=pltpu.SMEM), full],
        out_specs=[full, full],
        scratch_shapes=[pltpu.VMEM((800, 128), jnp.float32), pltpu.VMEM((832, 128), jnp.float32)],
        compiler_params=pltpu.CompilerParams(vmem_limit_bytes=VLIM),
        cost_estimate=pl.CostEstimate(flops=0, bytes_accessed=1_000_000, transcendentals=0),
        name="pack",
    )(scal, p)


def split_kernel(w_ref, h_ref, l_ref):
    n = pl.program_id(0)

    def body(j, last):
        x = w_ref[pl.ds(j, 160, stride=O), :]
        if last:
            lane = lax.broadcasted_iota(jnp.int32, x.shape, 1)
            x = jnp.where(lane < 32, x, 0.0)
        hi = x.astype(jnp.bfloat16)
        res = x - hi.astype(jnp.float32)
        m = pl.ds(pl.multiple_of(j * 128, 128), 128)
        t = pl.ds(pl.multiple_of(KMAIN + j * 32, 32), 32)
        if last:
            both = (hi.astype(jnp.float32) + pltpu.roll(res, 32, 1)).astype(jnp.bfloat16)
            h_ref[m, :] = both[:128]
            h_ref[t, :] = both[128:]
        else:
            lo = res.astype(jnp.bfloat16)
            h_ref[m, :] = hi[:128]
            h_ref[t, :] = hi[128:]
            l_ref[m, :] = lo[:128]
            l_ref[t, :] = lo[128:]

    @pl.when(n < 6)
    def _():
        pl.loop(0, O, unroll=2)(functools.partial(body, last=False))

    @pl.when(n == 6)
    def _():
        pl.loop(0, O, unroll=2)(functools.partial(body, last=True))


def split_weights(w):
    return pl.pallas_call(
        split_kernel,
        grid=(7,),
        out_shape=[
            jax.ShapeDtypeStruct((6400, 896), jnp.bfloat16),
            jax.ShapeDtypeStruct((6400, 768), jnp.bfloat16),
        ],
        in_specs=[pl.BlockSpec((6400, 128), lambda n: (0, n))],
        out_specs=[
            pl.BlockSpec((6400, 128), lambda n: (0, n)),
            pl.BlockSpec((6400, 128), lambda n: (0, jnp.minimum(n, 5))),
        ],
        compiler_params=pltpu.CompilerParams(vmem_limit_bytes=VLIM),
        cost_estimate=pl.CostEstimate(flops=20_000_000, bytes_accessed=44_000_000, transcendentals=0),
        name="split_w",
    )(w)


def product_kernel(places, slots, sc_ref, *refs):
    n_in = len(places)
    ins, (h_ref, l_ref), outs = refs[:n_in], refs[n_in : n_in + 2], refs[n_in + 2 : n_in + 6]
    a_s, t_s, lhs, hb, lb, acc1, acc2, zs, asem, wsem = refs[n_in + 6 :]
    x0, r0 = sc_ref[1], sc_ref[2]
    rows = 40 * slots
    mp = lhs.shape[0] // 2

    def wcopy(kb, buf):
        src = pl.ds(pl.multiple_of(kb * KBLK, KBLK), KBLK)
        return (
            pltpu.make_async_copy(h_ref.at[src], hb.at[buf], wsem.at[buf, 0]),
            pltpu.make_async_copy(l_ref.at[src], lb.at[buf], wsem.at[buf, 1]),
        )

    copies = []
    for op, where in zip(ins, places):
        for at, (slot, dx) in enumerate(where):
            x = lax.rem(x0 + dx, 4)
            copies.append(pltpu.make_async_copy(op.at[at, pl.ds(0, 50)], a_s.at[slot, pl.ds(50 * x, 50)], asem.at[0]))
            copies.append(pltpu.make_async_copy(op.at[at, pl.ds(50, 13)], t_s.at[slot, x], asem.at[1]))
    for c in copies:
        c.start()
    for c in wcopy(0, 0):
        c.start()
    for c in copies:
        c.wait()

    def put(at, parts):
        v = jnp.concatenate(parts, axis=0)
        if mp > rows:
            v = jnp.concatenate([v, jnp.zeros((mp - rows, 128), jnp.float32)], axis=0)
        hi = v.astype(jnp.bfloat16)
        lhs[0:mp, at * 128 : at * 128 + 128] = hi
        lhs[mp:, at * 128 : at * 128 + 128] = (v - hi.astype(jnp.float32)).astype(jnp.bfloat16)

    def block(kb, buf, first):
        for c in wcopy(kb, buf):
            c.wait()
        left = lhs[...]
        p1 = jnp.dot(left, hb[buf], preferred_element_type=jnp.float32)
        p2 = jnp.dot(left[:mp], lb[buf], preferred_element_type=jnp.float32)
        if first:
            acc1[...] = p1
            acc2[...] = p2
        else:
            acc1[...] += p1
            acc2[...] += p2

    acc1[...] = jnp.zeros_like(acc1)
    acc2[...] = jnp.zeros_like(acc2)

    @pl.loop(0, 4)
    def _(kb):
        buf = lax.rem(kb, 2)
        for c in wcopy(kb + 1, 1 - buf):
            c.start()
        for jj in range(10):
            j = kb * 10 + jj
            put(jj, [a_s[s, 40 * i + j] for s in range(slots) for i in range(5)])
        block(kb, buf, False)

    def tail_tile(s, t):
        if t == 12:
            return t_s[s, 0, 12] + t_s[s, 1, 0]
        if t == 37:
            return t_s[s, 2, 12] + t_s[s, 3, 0]
        if t < 12:
            return t_s[s, 0, t]
        if t < 25:
            return t_s[s, 1, t - 12]
        if t < 37:
            return t_s[s, 2, t - 25]
        return t_s[s, 3, t - 37]

    for g in range(10):
        put(g, [tail_tile(s, 10 * i + g) for s in range(slots) for i in range(5)])
    block(4, 0, False)

    n5 = 5 * slots
    for n in range(7):
        lanes = slice(128 * n, 128 * n + 128)
        z = acc1[0:rows, lanes] + acc1[mp : mp + rows, lanes]
        if n < 6:
            z = z + acc2[0:rows, lanes]
        else:
            z = z + pltpu.roll(acc1[0:rows, lanes], 96, 1)
        zs[n] = z
    for k, out in enumerate(outs):
        to = jnp.bitwise_xor(r0, k)
        for e in range(2):
            for n in range(7):
                wide = 128 if n < 6 else 32
                v = zs[n, pl.ds(2 * to + e, n5, stride=8), :]
                out[e * n5 : e * n5 + n5, 128 * n : 128 * n + wide] = v[:, :wide]


def product(scal, operands, places, slots, h, l):
    mp = -(-40 * slots // 16) * 16
    anyspec = pl.BlockSpec(memory_space=pl.ANY)
    f32, bf16 = jnp.float32, jnp.bfloat16
    return pl.pallas_call(
        functools.partial(product_kernel, places, slots),
        out_shape=[jax.ShapeDtypeStruct((10 * slots, 800), f32)] * 4,
        in_specs=[pl.BlockSpec(memory_space=pltpu.SMEM)] + [anyspec] * (len(operands) + 2),
        out_specs=[pl.BlockSpec(memory_space=pltpu.VMEM)] * 4,
        scratch_shapes=[
            pltpu.VMEM((slots, 200, 8, 128), f32),
            pltpu.VMEM((slots, 4, 13, 8, 128), f32),
            pltpu.VMEM((2 * mp, KBLK), bf16),
            pltpu.VMEM((2, KBLK, 896), bf16),
            pltpu.VMEM((2, KBLK, 768), bf16),
            pltpu.VMEM((2 * mp, 896), f32),
            pltpu.VMEM((mp, 768), f32),
            pltpu.VMEM((7, 40 * slots, 128), f32),
            pltpu.SemaphoreType.DMA((2,)),
            pltpu.SemaphoreType.DMA((2, 2)),
        ],
        compiler_params=pltpu.CompilerParams(vmem_limit_bytes=VLIM),
        cost_estimate=pl.CostEstimate(flops=40 * slots * 6400 * 800 * 6, bytes_accessed=22_000_000, transcendentals=0),
        name="product",
    )(scal, *operands, h, l)


def place_kernel(chunks, sc_ref, *refs):
    o_ref, o_s = refs[-2], refs[-1]
    z0, y0 = sc_ref[3], sc_ref[4]
    for c, slots in enumerate(chunks):
        n5 = 5 * len(slots)
        a, b, d, e = (refs[4 * c + k][...] for k in range(4))
        v = (a + b) + (d + e)
        for half_e in range(2):
            for s, (h, dz, dy) in enumerate(slots):
                g = 2 * lax.rem(z0 + dz, 4) + lax.rem(y0 + dy, 2)
                at = half_e * n5 + 5 * s
                o_s[2 * h + half_e, g, 0:5, :] = v[at : at + 5, :]
    for a2 in range(4):
        for g in range(8):
            o_ref[40 * a2 + 5 * g : 40 * a2 + 5 * g + 5, :] = o_s[a2, g, 0:5, :]


def place(scal, chunks, arrays):
    full = pl.BlockSpec(memory_space=pltpu.VMEM)
    return pl.pallas_call(
        functools.partial(place_kernel, chunks),
        out_shape=jax.ShapeDtypeStruct((160, 800), jnp.float32),
        in_specs=[pl.BlockSpec(memory_space=pltpu.SMEM)] + [full] * len(arrays),
        out_specs=full,
        scratch_shapes=[pltpu.VMEM((4, 8, 8, 800), jnp.float32)],
        compiler_params=pltpu.CompilerParams(vmem_limit_bytes=VLIM),
        cost_estimate=pl.CostEstimate(flops=1_000_000, bytes_accessed=3_000_000, transcendentals=0),
        name="place",
    )(scal, *arrays)


def cidx(z, y, x):
    return (z % 4) * 8 + (y % 2) * 4 + x % 4


def shift(dz=0, dy=0, dx=0):
    return [(cidx(z, y, x), cidx(z + dz, y + dy, x + dx)) for z in range(4) for y in range(2) for x in range(4)]


XP, XM, ZP, ZM, YY = shift(dx=1), shift(dx=-1), shift(dz=1), shift(dz=-1), shift(dy=1)


def send(v, perm):
    return lax.ppermute(v, "col", perm)


def after(v, *others):
    return lax.optimization_barrier((v, *others))[0]


def to_peers(outs):
    return [outs[0]] + [lax.ppermute(outs[k], "row", [(r, r ^ k) for r in range(4)]) for k in (1, 2, 3)]


def per_device(pair_amps, cycle_w):
    c, r = lax.axis_index("col"), lax.axis_index("row")
    x0, y0, z0 = c % 4, (c // 4) % 2, c // 8
    scal = jnp.stack([c % 2, x0, r, z0, y0]).astype(jnp.int32)
    pay0, pay1 = pack(scal, pair_amps)
    pay0, pay1 = pay0.reshape(1, PAY, 8, 128), pay1.reshape(1, PAY, 8, 128)

    fm0, fp0 = send(pay0, XP), send(pay0, XM)
    fm1, fp1 = send(pay1, ZP), send(pay1, ZM)
    w0 = jnp.concatenate([send(fm0[:, :32], XP), send(fp0[:, 32:], XM)], axis=1)
    w1 = jnp.concatenate([send(fm1[:, :32], ZP), send(fp1[:, 32:], ZM)], axis=1)
    g0 = jnp.concatenate([pay0, fm0, fp0, w0], axis=0)
    c1 = jnp.concatenate([pay1, fm1], axis=0), jnp.concatenate([fp1, w1], axis=0)
    g1 = jnp.concatenate([*c1], axis=0)

    y1a = send(c1[0], YY)
    y0g = send(after(g0, y1a), YY)
    y1b = send(after(c1[1], y0g), YY)

    zm, zp = send(g0, ZP), send(g0, ZM)
    xm, xp = send(g1, XP), send(g1, XM)
    wl = after(cycle_w, g0, g1)
    wh, wlo = split_weights(wl)
    zf, zb = send(zm[:2], ZP), send(zp[2:], ZM)
    xf, xb = send(xm[:2], XP), send(xp[2:], XM)

    yzm, yzp = send(after(y0g, zf), ZP), send(after(y0g, zb), ZM)
    yxm0, yxp0 = send(after(y1a, xf), XP), send(after(y1a, xb), XM)
    yxm1, yxp1 = send(after(y1b, yxm0), XP), send(after(y1b, yxp0), XM)
    yzf, yzb = send(yzm[:2], ZP), send(yzp[2:], ZM)
    yxf, yxb = send(after(yxm0, yxm1), XP), send(yxp1, XM)

    dxs = (0, 3, 1, 2)
    row = lambda s: [(s, d) for d in dxs]
    col = lambda d, n=4, s0=0: [(s0 + s, d) for s in range(n)]

    oa = product(scal, [g0, zm, zp, zf, zb, y0g], [row(0), row(1), row(2), row(3)[:2], row(3)[2:], row(4)], 5, wh, wlo)
    sa = [(0, 0, 0), (0, 3, 0), (0, 1, 0), (0, 2, 0), (0, 0, 1)]
    ob = product(scal, [g1, xm, xp, xf, xb], [col(0), col(3), col(1), col(2, 2), col(2, 2, 2)], 4, wh, wlo)
    sb = [(1, 0, 0), (1, 3, 0), (1, 1, 0), (1, 2, 0)]
    oc = product(scal, [yzm, yzp], [row(0), row(1)], 2, wh, wlo)
    sc = [(0, 3, 1), (0, 1, 1)]
    od = product(
        scal,
        [yzf, yzb, y1a, y1b, yxm0, yxm1, yxp0, yxp1, yxf, yxb],
        [row(0)[:2], row(0)[2:], col(0, 2, 1), col(0, 2, 3), col(3, 2, 1), col(3, 2, 3), col(1, 2, 1), col(1, 2, 3), col(2, 2, 1), col(2, 2, 3)],
        5,
        wh,
        wlo,
    )
    sd = [(0, 2, 1), (1, 0, 1), (1, 3, 1), (1, 1, 1), (1, 2, 1)]
    return place(scal, (sa, sb, sc, sd), [v for o in (oa, ob, oc, od) for v in to_peers(o)])


def solution(mesh):
    return jax.shard_map(
        per_device,
        mesh=mesh,
        in_specs=(P("row", "col"), P("row", "col")),
        out_specs=P("row", "col"),
        check_vma=False,
    )
```

```python
import functools

import jax
import jax.numpy as jnp
from jax import lax
from jax.experimental import pallas as pl
from jax.experimental.pallas import tpu as pltpu
from jax.sharding import PartitionSpec as P

O = 40
PAY = 63
KMAIN, KTAIL = 5120, 1280
KBLK = 1280
VLIM = 16 * 1024 * 1024
SPLIT_VLIM = 28 * 1024 * 1024
ORDER = (6, 0, 1, 2, 3, 4, 5)


def pack_kernel(sc_ref, p_ref, o0_ref, o1_ref, main, tail):
    base = pl.multiple_of(sc_ref[0] * 32, 32)
    tail[...] = jnp.zeros_like(tail)
    for k in range(7):
        if k < 6:
            x = p_ref[:, 128 * k : 128 * k + 128]
            rows = 128
        else:
            x = jnp.concatenate([p_ref[:, 768:800], jnp.zeros((160, 96), jnp.float32)], axis=1)
            rows = 32
        x = jnp.concatenate([x, jnp.zeros((96, 128), jnp.float32)], axis=0)
        xt = x.T
        main[128 * k : 128 * k + rows, :] = xt[:rows, :128]
        tail[pl.ds(base + 128 * k, rows), :] = xt[:rows, 128:]
    for h, o_ref in ((0, o0_ref), (1, o1_ref)):
        for s in range(8):
            a = 4 * (s // 2) + 2 * h + s % 2
            o_ref[pl.ds(s, 50, stride=8), :] = main[pl.ds(a, 50, stride=16), :]
            t = tail[pl.ds(a, 13, stride=64), :]
            for q in range(1, 4):
                t = t + pltpu.roll(tail[pl.ds(16 * q + a, 13, stride=64), :], 32 * q, 1)
            o_ref[pl.ds(400 + s, 13, stride=8), :] = t


def pack(scal, p):
    full = pl.BlockSpec(memory_space=pltpu.VMEM)
    return pl.pallas_call(
        pack_kernel,
        out_shape=[jax.ShapeDtypeStruct((PAY * 8, 128), jnp.float32)] * 2,
        in_specs=[pl.BlockSpec(memory_space=pltpu.SMEM), full],
        out_specs=[full, full],
        scratch_shapes=[pltpu.VMEM((800, 128), jnp.float32), pltpu.VMEM((832, 128), jnp.float32)],
        compiler_params=pltpu.CompilerParams(vmem_limit_bytes=VLIM),
        cost_estimate=pl.CostEstimate(flops=0, bytes_accessed=1_000_000, transcendentals=0),
        name="pack",
    )(scal, p)


def join_kernel(counts, *refs):
    ins, outs = refs[: sum(counts)], refs[sum(counts) :]
    for out, count in zip(outs, counts):
        at = 0
        for ref in ins[:count]:
            out[at : at + ref.shape[0]] = ref[...]
            at += ref.shape[0]
        ins = ins[count:]


def join(*groups):
    vmem = pl.BlockSpec(memory_space=pltpu.VMEM)
    flat = [v for group in groups for v in group]
    return pl.pallas_call(
        functools.partial(join_kernel, [len(group) for group in groups]),
        out_shape=[jax.ShapeDtypeStruct((sum(v.shape[0] for v in g), PAY, 8, 128), jnp.float32) for g in groups],
        in_specs=[vmem] * len(flat),
        out_specs=[vmem] * len(groups),
        compiler_params=pltpu.CompilerParams(vmem_limit_bytes=VLIM),
        cost_estimate=pl.CostEstimate(flops=0, bytes_accessed=1_000_000, transcendentals=0),
        name="join",
    )(*flat)


NA, NB = 256, 512
WIDE_A, WIDE_B = 2 * NA, 2 * NB + 128


def split_kernel(wt_ref, a_ref, b_ref, tok_ref, buf, tr, sem):
    def fetch(at):
        n = ORDER[at]
        rows = 128 if n < 6 else 32
        return pltpu.make_async_copy(wt_ref.at[pl.ds(128 * n, rows)], buf.at[at % 2, pl.ds(0, rows)], sem.at[at % 2])

    def turn(at, kt):
        k = pl.ds(pl.multiple_of(kt * 128, 128), 128)
        if ORDER[at] < 6:
            tr[at % 2, k, :] = buf[at % 2, :, k].T
        else:
            tr[at % 2, k, 0:32] = buf[at % 2, 0:32, k].T

    def store(at, j):
        n = ORDER[at]
        o_ref = a_ref if n < 2 else b_ref
        hi_at = 128 * n if n < 2 else 128 * (n - 2)
        lo_at = hi_at + (NA if n < 2 else NB + 128)
        x = tr[at % 2, pl.ds(j, 160, stride=O), :]
        if n == 6:
            lane = lax.broadcasted_iota(jnp.int32, x.shape, 1)
            x = jnp.where(lane < 32, x, 0.0)
        hi = x.astype(jnp.bfloat16)
        res = x - hi.astype(jnp.float32)
        m = pl.ds(pl.multiple_of(j * 128, 128), 128)
        t = pl.ds(pl.multiple_of(KMAIN + j * 32, 32), 32)
        if n == 6:
            hi = (hi.astype(jnp.float32) + pltpu.roll(res, 32, 1)).astype(jnp.bfloat16)
        o_ref[m, hi_at : hi_at + 128] = hi[:128]
        o_ref[t, hi_at : hi_at + 128] = hi[128:]
        if n < 6:
            lo = res.astype(jnp.bfloat16)
            o_ref[m, lo_at : lo_at + 128] = lo[:128]
            o_ref[t, lo_at : lo_at + 128] = lo[128:]

    count = len(ORDER)
    fetch(0).start()
    for at in range(count + 1):
        if at + 1 < count:
            fetch(at + 1).start()
        if at < count:
            fetch(at).wait()

        @pl.loop(0, 5)
        def _(u):
            if at < count:
                for v in range(10):
                    turn(at, 10 * u + v)
            if at > 0:
                for v in range(8):
                    store(at - 1, 8 * u + v)

    tok_ref[...] = jnp.zeros_like(tok_ref)


def split_weights(wt):
    vmem = pl.BlockSpec(memory_space=pltpu.VMEM)
    return pl.pallas_call(
        split_kernel,
        out_shape=[
            jax.ShapeDtypeStruct((6400, WIDE_A), jnp.bfloat16),
            jax.ShapeDtypeStruct((6400, WIDE_B), jnp.bfloat16),
            jax.ShapeDtypeStruct((8, 128), jnp.float32),
        ],
        in_specs=[pl.BlockSpec(memory_space=pltpu.HBM)],
        out_specs=[vmem, vmem, vmem],
        scratch_shapes=[
            pltpu.VMEM((2, 128, 6400), jnp.float32),
            pltpu.VMEM((2, 6400, 128), jnp.float32),
            pltpu.SemaphoreType.DMA((2,)),
        ],
        compiler_params=pltpu.CompilerParams(vmem_limit_bytes=SPLIT_VLIM),
        cost_estimate=pl.CostEstimate(flops=0, bytes_accessed=45_000_000, transcendentals=0),
        name="split_w",
    )(wt)


def product_kernel(places, slots, carried, sc_ref, *refs):
    n_in = len(refs) - 9 - (3 if carried else 0)
    ins, (wa, wb) = refs[:n_in], refs[n_in : n_in + 2]
    before, outs = refs[n_in + 2 : -7], refs[-7:-4]
    lhs, acc1, acc2, zs = refs[-4:]
    x0, r0 = sc_ref[1], sc_ref[2]
    rows = 40 * slots
    mp = lhs.shape[0] // 2

    def put(at, parts):
        v = jnp.concatenate(parts, axis=0)
        if mp > rows:
            v = jnp.concatenate([v, jnp.zeros((mp - rows, 128), jnp.float32)], axis=0)
        hi = v.astype(jnp.bfloat16)
        lhs[0:mp, at * 128 : at * 128 + 128] = hi
        lhs[mp:, at * 128 : at * 128 + 128] = (v - hi.astype(jnp.float32)).astype(jnp.bfloat16)

    def fill(kb, at_x):
        def tile(s, x, t):
            op, at = places[s](at_x, x)
            return ins[op][at, t]

        def tail(s, t):
            if t == 12:
                return tile(s, 0, 62) + tile(s, 1, 50)
            if t == 37:
                return tile(s, 2, 62) + tile(s, 3, 50)
            x, lo = (0, 0) if t < 12 else (1, 12) if t < 25 else (2, 25) if t < 37 else (3, 37)
            return tile(s, x, 50 + t - lo)

        for jj in range(10):
            if kb < 4:
                parts = [tile(s, (4 * i + kb) // 5, 10 * ((4 * i + kb) % 5) + jj) for s in range(slots) for i in range(5)]
            else:
                parts = [tail(s, 10 * i + jj) for s in range(slots) for i in range(5)]
            put(jj, parts)

    dot = functools.partial(jnp.dot, preferred_element_type=jnp.float32)
    for kb in range(5):
        for at_x in range(4):
            pl.when(x0 == at_x)(functools.partial(fill, kb, at_x))
        k = slice(kb * KBLK, kb * KBLK + KBLK)
        one = dot(lhs[...], wa[k, 0:NA]), dot(lhs[...], wb[k, 0 : NB + 128])
        two = dot(lhs[0:mp], wa[k, NA:]), dot(lhs[0:mp], wb[k, NB + 128 :])
        if kb == 0:
            acc1[:, 0:NA], acc1[:, NA:] = one
            acc2[:, 0:NA], acc2[:, NA:] = two
        else:
            acc1[:, 0:NA] += one[0]
            acc1[:, NA:] += one[1]
            acc2[:, 0:NA] += two[0]
            acc2[:, NA:] += two[1]

    n5 = 5 * slots
    for n in range(7):
        lanes = slice(128 * n, 128 * n + 128)
        z = acc1[0:rows, lanes] + acc1[mp : mp + rows, lanes]
        if n < 6:
            z = z + acc2[0:rows, lanes]
        else:
            z = z + pltpu.roll(acc1[0:rows, lanes], 96, 1)
        zs[n] = z
    for out, at, k in ((0, 0, 0), (1, 0, 2), (2, 0, 1), (2, carried + 2 * n5, 3)):
        to = jnp.bitwise_xor(r0, k)
        if carried:
            have = slice(carried, 2 * carried) if k == 3 else slice(0, carried)
            outs[out][at : at + carried, :] = before[out][have, :]
            at += carried
        for e in range(2):
            for n in range(7):
                wide = 128 if n < 6 else 32
                v = zs[n, pl.ds(2 * to + e, n5, stride=8), :]
                outs[out][at + e * n5 : at + e * n5 + n5, 128 * n : 128 * n + wide] = v[:, :wide]


def product(scal, operands, places, w, before=()):
    slots = len(places)
    carried = before[0].shape[0] if before else 0
    mp = -(-40 * slots // 16) * 16
    f32, bf16 = jnp.float32, jnp.bfloat16
    vmem = pl.BlockSpec(memory_space=pltpu.VMEM)
    return pl.pallas_call(
        functools.partial(product_kernel, places, slots, carried),
        out_shape=[jax.ShapeDtypeStruct((k * (carried + 10 * slots), 800), f32) for k in (1, 1, 2)],
        in_specs=[pl.BlockSpec(memory_space=pltpu.SMEM)] + [vmem] * (len(operands) + 2 + len(before)),
        out_specs=[vmem] * 3,
        scratch_shapes=[
            pltpu.VMEM((2 * mp, KBLK), bf16),
            pltpu.VMEM((2 * mp, 896), f32),
            pltpu.VMEM((mp, 768), f32),
            pltpu.VMEM((7, 40 * slots, 128), f32),
        ],
        compiler_params=pltpu.CompilerParams(vmem_limit_bytes=VLIM),
        cost_estimate=pl.CostEstimate(flops=40 * slots * 6400 * 800 * 6, bytes_accessed=22_000_000, transcendentals=0),
        name="product",
    )(scal, *operands, *w, *before)


def place_kernel(chunks, sc_ref, *refs):
    o_ref, o_s = refs[-2], refs[-1]
    z0, y0 = sc_ref[3], sc_ref[4]
    for c, parts in enumerate(chunks):
        mine, core, across = refs[3 * c : 3 * c + 3]
        v = mine[...] + core[0 : mine.shape[0]] + across[...]
        base = 0
        for slots in parts:
            n5 = 5 * len(slots)
            for half_e in range(2):
                for s, (h, z_of, dy) in enumerate(slots):
                    g = 2 * z_of(z0) + lax.rem(y0 + dy, 2)
                    at = base + half_e * n5 + 5 * s
                    o_s[2 * h + half_e, g, 0:5, :] = v[at : at + 5, :]
            base += 2 * n5
    for a2 in range(4):
        for g in range(8):
            o_ref[40 * a2 + 5 * g : 40 * a2 + 5 * g + 5, :] = o_s[a2, g, 0:5, :]


def place(scal, chunks, arrays):
    full = pl.BlockSpec(memory_space=pltpu.VMEM)
    return pl.pallas_call(
        functools.partial(place_kernel, chunks),
        out_shape=jax.ShapeDtypeStruct((160, 800), jnp.float32),
        in_specs=[pl.BlockSpec(memory_space=pltpu.SMEM)] + [full] * len(arrays),
        out_specs=full,
        scratch_shapes=[pltpu.VMEM((4, 8, 8, 800), jnp.float32)],
        compiler_params=pltpu.CompilerParams(vmem_limit_bytes=VLIM),
        cost_estimate=pl.CostEstimate(flops=1_000_000, bytes_accessed=3_000_000, transcendentals=0),
        name="place",
    )(scal, *arrays)


def cidx(z, y, x):
    return (z % 4) * 8 + (y % 2) * 4 + x % 4


def shift(dz=0, dy=0, dx=0):
    return [(cidx(z, y, x), cidx(z + dz, y + dy, x + dx)) for z in range(4) for y in range(2) for x in range(4)]


XP, XM, ZP, ZM, YY = shift(dx=1), shift(dx=-1), shift(dz=1), shift(dz=-1), shift(dy=1)
X2, Z2 = shift(dx=2), shift(dz=2)


def send(v, perm):
    return lax.ppermute(v, "col", perm)


def after(v, *others):
    return lax.optimization_barrier((v, *others))[0]


def to_core(outs):
    return lax.ppermute(outs[2], "row", [(r, r ^ 1) for r in range(4)])


def to_partner(outs, got):
    rows = outs[1].shape[0]
    return lax.ppermute(outs[1] + got[rows:], "row", [(r, r ^ 2) for r in range(4)])


def per_device(pair_amps, cycle_w):
    c, r = lax.axis_index("col"), lax.axis_index("row")
    x0, y0, z0 = c % 4, (c // 4) % 2, c // 8
    scal = jnp.stack([c % 2, x0, r, z0, y0]).astype(jnp.int32)
    wt = cycle_w.T
    pay0, pay1 = pack(scal, pair_amps)
    pay0, pay1 = pay0.reshape(1, PAY, 8, 128), pay1.reshape(1, PAY, 8, 128)

    m0, m1 = send(pay0, XP), send(pay1, ZP)
    p0, p1 = send(pay0, XM), send(pay1, ZM)
    f0, f1 = send(pay0, X2), send(pay1, Z2)
    g0, g1 = join((pay0, m0, p0, f0), (pay1, m1, p1, f1))

    zm, zp = send(g0, ZP), send(g0, ZM)
    xm, xp = send(g1, XP), send(g1, XM)
    y0g = send(g0, YY)
    *w, tok_b = split_weights(after(wt, g0))
    zm, zp, xm, xp, y0g = (after(v, tok_b) for v in (zm, zp, xm, xp, y0g))
    zf, zb = send(zm[:2], ZP), send(zp[2:], ZM)
    xf, xb = send(xm[:2], XP), send(xp[2:], XM)
    y1g = send(after(g1, y0g), YY)

    yzm, yzp = send(after(y0g, zf), ZP), send(after(y0g, zb), ZM)
    yxm, yxp = send(after(y1g, xf), XP), send(after(y1g, xb), XM)

    whole = lambda op: lambda own, x: (op, (0, 2, 3, 1)[(x - own) % 4])
    halves = lambda lo, hi: lambda own, x: ((lo, 0), (hi, 0), (hi, 1), (lo, 1))[(x - own) % 4]
    ring = lambda s, of: lambda own, x: of[(x - own) % 4](s)
    plus = lambda dz: lambda z: lax.rem(z + dz, 4)
    column = (0, 3, 1, 2)
    of = [lambda s: (6, s), lambda s: (8, s), lambda s: (9 + s // 2, s % 2), lambda s: (7, s)]
    oa = product(
        scal,
        [g0, zm, zp, zf, zb, y0g, g1, xm, xp, xf, xb],
        [whole(0), whole(1), whole(2), halves(3, 4), whole(5)] + [ring(s, of) for s in range(4)],
        w,
    )
    sa = [(0, plus(d), 0) for d in column] + [(0, plus(0), 1)] + [(1, plus(d), 0) for d in column]
    yzm, yzp, yxm, yxp = (after(v, oa[0]) for v in (yzm, yzp, yxm, yxp))
    yzf, yzb = send(yzm[:2], ZP), send(yzp[2:], ZM)
    yxf, yxb = send(yxm[:2], XP), send(yxp[2:], XM)
    got_a = to_core(oa)
    ob = product(scal, [after(yzm, got_a), yzp], [whole(0), whole(1)], w)
    sb = [(0, plus(3), 1), (0, plus(1), 1)]
    sums_a = [oa[0], got_a, to_partner(oa, got_a)]
    yzf = after(yzf, ob[0], sums_a[2])
    of = [lambda s: (2, s), lambda s: (4, s), lambda s: (5 + s // 2, s % 2), lambda s: (3, s)]
    oc = product(
        scal, [yzf, yzb, y1g, yxm, yxp, yxf, yxb], [halves(0, 1)] + [ring(s, of) for s in range(4)], w, ob
    )
    sc = [(0, plus(2), 1)] + [(1, plus(d), 1) for d in column]
    got_c = to_core(oc)
    sums_c = [oc[0], got_c, to_partner(oc, got_c)]
    return place(scal, ((sa,), (sb, sc)), sums_a + sums_c)


def solution(mesh):
    return jax.shard_map(
        per_device,
        mesh=mesh,
        in_specs=(P("row", "col"), P("row", "col")),
        out_specs=P("row", "col"),
        check_vma=False,
    )
```

```python
import functools

import jax
import jax.numpy as jnp
from jax import lax
from jax.experimental import pallas as pl
from jax.experimental.pallas import tpu as pltpu
from jax.sharding import PartitionSpec as P

O = 40
PAY = 63
KMAIN, KTAIL = 5120, 1280
KBLK = 1280
VLIM = 16 * 1024 * 1024
SPLIT_VLIM = 28 * 1024 * 1024
ORDER = (6, 0, 1, 2, 3, 4, 5)


def pack_kernel(sc_ref, p_ref, o0_ref, o1_ref, main, tail):
    base = pl.multiple_of(sc_ref[0] * 32, 32)
    tail[...] = jnp.zeros_like(tail)
    for k in range(7):
        if k < 6:
            x = p_ref[:, 128 * k : 128 * k + 128]
            rows = 128
        else:
            x = jnp.concatenate([p_ref[:, 768:800], jnp.zeros((160, 96), jnp.float32)], axis=1)
            rows = 32
        x = jnp.concatenate([x, jnp.zeros((96, 128), jnp.float32)], axis=0)
        xt = x.T
        main[128 * k : 128 * k + rows, :] = xt[:rows, :128]
        tail[pl.ds(base + 128 * k, rows), :] = xt[:rows, 128:]
    for h, o_ref in ((0, o0_ref), (1, o1_ref)):
        for s in range(8):
            a = 4 * (s // 2) + 2 * h + s % 2
            o_ref[pl.ds(s, 50, stride=8), :] = main[pl.ds(a, 50, stride=16), :]
            t = tail[pl.ds(a, 13, stride=64), :]
            for q in range(1, 4):
                t = t + pltpu.roll(tail[pl.ds(16 * q + a, 13, stride=64), :], 32 * q, 1)
            o_ref[pl.ds(400 + s, 13, stride=8), :] = t


def pack(scal, p):
    full = pl.BlockSpec(memory_space=pltpu.VMEM)
    return pl.pallas_call(
        pack_kernel,
        out_shape=[jax.ShapeDtypeStruct((PAY * 8, 128), jnp.float32)] * 2,
        in_specs=[pl.BlockSpec(memory_space=pltpu.SMEM), full],
        out_specs=[full, full],
        scratch_shapes=[pltpu.VMEM((800, 128), jnp.float32), pltpu.VMEM((832, 128), jnp.float32)],
        compiler_params=pltpu.CompilerParams(vmem_limit_bytes=VLIM),
        cost_estimate=pl.CostEstimate(flops=0, bytes_accessed=1_000_000, transcendentals=0),
        name="pack",
    )(scal, p)


def join_kernel(lists, *refs):
    ins, outs = refs[: -len(lists)], refs[-len(lists) :]
    for out, which in zip(outs, lists):
        at = 0
        for k in which:
            out[at : at + ins[k].shape[0]] = ins[k][...]
            at += ins[k].shape[0]


def join(arrays, *lists):
    vmem = pl.BlockSpec(memory_space=pltpu.VMEM)
    return pl.pallas_call(
        functools.partial(join_kernel, lists),
        out_shape=[
            jax.ShapeDtypeStruct((sum(arrays[k].shape[0] for k in which), PAY, 8, 128), jnp.float32) for which in lists
        ],
        in_specs=[vmem] * len(arrays),
        out_specs=[vmem] * len(lists),
        compiler_params=pltpu.CompilerParams(vmem_limit_bytes=VLIM),
        cost_estimate=pl.CostEstimate(flops=0, bytes_accessed=1_000_000, transcendentals=0),
        name="join",
    )(*arrays)


NA, NB = 256, 512
WIDE_A, WIDE_B = 2 * NA, 2 * NB + 128


def split_kernel(wt_ref, a_ref, b_ref, tok_ref, buf, tr, sem):
    def fetch(at):
        n = ORDER[at]
        rows = 128 if n < 6 else 32
        return pltpu.make_async_copy(wt_ref.at[pl.ds(128 * n, rows)], buf.at[at % 2, pl.ds(0, rows)], sem.at[at % 2])

    def turn(at, kt):
        k = pl.ds(pl.multiple_of(kt * 128, 128), 128)
        if ORDER[at] < 6:
            tr[at % 2, k, :] = buf[at % 2, :, k].T
        else:
            tr[at % 2, k, 0:32] = buf[at % 2, 0:32, k].T

    def store(at, j):
        n = ORDER[at]
        o_ref = a_ref if n < 2 else b_ref
        hi_at = 128 * n if n < 2 else 128 * (n - 2)
        lo_at = hi_at + (NA if n < 2 else NB + 128)
        x = tr[at % 2, pl.ds(j, 160, stride=O), :]
        if n == 6:
            lane = lax.broadcasted_iota(jnp.int32, x.shape, 1)
            x = jnp.where(lane < 32, x, 0.0)
        hi = x.astype(jnp.bfloat16)
        res = x - hi.astype(jnp.float32)
        m = pl.ds(pl.multiple_of(j * 128, 128), 128)
        t = pl.ds(pl.multiple_of(KMAIN + j * 32, 32), 32)
        if n == 6:
            hi = (hi.astype(jnp.float32) + pltpu.roll(res, 32, 1)).astype(jnp.bfloat16)
        o_ref[m, hi_at : hi_at + 128] = hi[:128]
        o_ref[t, hi_at : hi_at + 128] = hi[128:]
        if n < 6:
            lo = res.astype(jnp.bfloat16)
            o_ref[m, lo_at : lo_at + 128] = lo[:128]
            o_ref[t, lo_at : lo_at + 128] = lo[128:]

    count = len(ORDER)
    fetch(0).start()
    for at in range(count + 1):
        if at + 1 < count:
            fetch(at + 1).start()
        if at < count:
            fetch(at).wait()

        @pl.loop(0, 5)
        def _(u):
            if at < count:
                for v in range(10):
                    turn(at, 10 * u + v)
            if at > 0:
                for v in range(8):
                    store(at - 1, 8 * u + v)

    tok_ref[...] = jnp.zeros_like(tok_ref)


def split_weights(wt):
    vmem = pl.BlockSpec(memory_space=pltpu.VMEM)
    return pl.pallas_call(
        split_kernel,
        out_shape=[
            jax.ShapeDtypeStruct((6400, WIDE_A), jnp.bfloat16),
            jax.ShapeDtypeStruct((6400, WIDE_B), jnp.bfloat16),
            jax.ShapeDtypeStruct((8, 128), jnp.float32),
        ],
        in_specs=[pl.BlockSpec(memory_space=pltpu.HBM)],
        out_specs=[vmem, vmem, vmem],
        scratch_shapes=[
            pltpu.VMEM((2, 128, 6400), jnp.float32),
            pltpu.VMEM((2, 6400, 128), jnp.float32),
            pltpu.SemaphoreType.DMA((2,)),
        ],
        compiler_params=pltpu.CompilerParams(vmem_limit_bytes=SPLIT_VLIM),
        cost_estimate=pl.CostEstimate(flops=0, bytes_accessed=45_000_000, transcendentals=0),
        name="split_w",
    )(wt)


def lines_at(own, late):
    first = 5 * ((own + 2) % 4) // 4
    return [first, first + 1] if late else [i for i in range(5) if i not in (first, first + 1)]


def product_kernel(places, carried, sc_ref, *refs):
    n_in = len(refs) - 9 - (3 if carried else 0)
    ins, (wa, wb) = refs[:n_in], refs[n_in : n_in + 2]
    before, outs = refs[n_in + 2 : -7], refs[-7:-4]
    lhs, acc1, acc2, zs = refs[-4:]
    x0, r0 = sc_ref[1], sc_ref[2]
    slots = len(places)
    n5 = sum(len(lines(0)) for _, lines in places)
    rows = 8 * n5
    mp = lhs.shape[0] // 2

    def put(at, parts):
        v = jnp.concatenate(parts, axis=0)
        if mp > rows:
            v = jnp.concatenate([v, jnp.zeros((mp - rows, 128), jnp.float32)], axis=0)
        hi = v.astype(jnp.bfloat16)
        lhs[0:mp, at * 128 : at * 128 + 128] = hi
        lhs[mp:, at * 128 : at * 128 + 128] = (v - hi.astype(jnp.float32)).astype(jnp.bfloat16)

    def fill(kb, at_x):
        def tile(s, x, t):
            op, at = places[s][0](at_x, x)
            return ins[op][at, t]

        def tail(s, t):
            if t == 12:
                return tile(s, 0, 62) + tile(s, 1, 50)
            if t == 37:
                return tile(s, 2, 62) + tile(s, 3, 50)
            x, lo = (0, 0) if t < 12 else (1, 12) if t < 25 else (2, 25) if t < 37 else (3, 37)
            return tile(s, x, 50 + t - lo)

        for jj in range(10):
            if kb < 4:
                parts = [tile(s, (4 * i + kb) // 5, 10 * ((4 * i + kb) % 5) + jj) for s in range(slots) for i in places[s][1](at_x)]
            else:
                parts = [tail(s, 10 * i + jj) for s in range(slots) for i in places[s][1](at_x)]
            put(jj, parts)

    dot = functools.partial(jnp.dot, preferred_element_type=jnp.float32)
    for kb in range(5):
        for at_x in range(4):
            pl.when(x0 == at_x)(functools.partial(fill, kb, at_x))
        k = slice(kb * KBLK, kb * KBLK + KBLK)
        one = dot(lhs[...], wa[k, 0:NA]), dot(lhs[...], wb[k, 0 : NB + 128])
        two = dot(lhs[0:mp], wa[k, NA:]), dot(lhs[0:mp], wb[k, NB + 128 :])
        if kb == 0:
            acc1[:, 0:NA], acc1[:, NA:] = one
            acc2[:, 0:NA], acc2[:, NA:] = two
        else:
            acc1[:, 0:NA] += one[0]
            acc1[:, NA:] += one[1]
            acc2[:, 0:NA] += two[0]
            acc2[:, NA:] += two[1]

    for n in range(7):
        lanes = slice(128 * n, 128 * n + 128)
        z = acc1[0:rows, lanes] + acc1[mp : mp + rows, lanes]
        if n < 6:
            z = z + acc2[0:rows, lanes]
        else:
            z = z + pltpu.roll(acc1[0:rows, lanes], 96, 1)
        zs[n] = z
    for out, at, k in ((0, 0, 0), (1, 0, 2), (2, 0, 1), (2, carried + 2 * n5, 3)):
        to = jnp.bitwise_xor(r0, k)
        if carried:
            have = slice(carried, 2 * carried) if k == 3 else slice(0, carried)
            outs[out][at : at + carried, :] = before[out][have, :]
            at += carried
        for e in range(2):
            for n in range(7):
                wide = 128 if n < 6 else 32
                v = zs[n, pl.ds(2 * to + e, n5, stride=8), :]
                outs[out][at + e * n5 : at + e * n5 + n5, 128 * n : 128 * n + wide] = v[:, :wide]


def product(scal, operands, places, w, before=()):
    n5 = sum(len(lines(0)) for _, lines in places)
    carried = before[0].shape[0] if before else 0
    mp = -(-8 * n5 // 16) * 16
    f32, bf16 = jnp.float32, jnp.bfloat16
    vmem = pl.BlockSpec(memory_space=pltpu.VMEM)
    return pl.pallas_call(
        functools.partial(product_kernel, places, carried),
        out_shape=[jax.ShapeDtypeStruct((k * (carried + 2 * n5), 800), f32) for k in (1, 1, 2)],
        in_specs=[pl.BlockSpec(memory_space=pltpu.SMEM)] + [vmem] * (len(operands) + 2 + len(before)),
        out_specs=[vmem] * 3,
        scratch_shapes=[
            pltpu.VMEM((2 * mp, KBLK), bf16),
            pltpu.VMEM((2 * mp, 896), f32),
            pltpu.VMEM((mp, 768), f32),
            pltpu.VMEM((7, 8 * n5, 128), f32),
        ],
        compiler_params=pltpu.CompilerParams(vmem_limit_bytes=VLIM),
        cost_estimate=pl.CostEstimate(flops=8 * n5 * 6400 * 800 * 6, bytes_accessed=22_000_000, transcendentals=0),
        name="product",
    )(scal, *operands, *w, *before)


def place_kernel(chunks, sc_ref, *refs):
    o_ref, o_s = refs[-2], refs[-1]
    x0, z0, y0 = sc_ref[1], sc_ref[3], sc_ref[4]

    def put(v, at_x, parts):
        at = 0
        for slots in parts:
            for half_e in range(2):
                for h, z_of, dy, lines in slots:
                    g = 2 * z_of(z0) + lax.rem(y0 + dy, 2)
                    for i in lines(at_x):
                        o_s[2 * h + half_e, g, i : i + 1, :] = v[at : at + 1, :]
                        at += 1

    for c, parts in enumerate(chunks):
        mine, core, across = refs[3 * c : 3 * c + 3]
        v = mine[...] + core[0 : mine.shape[0]] + across[...]
        for at_x in range(4):
            pl.when(x0 == at_x)(functools.partial(put, v, at_x, parts))
    for a2 in range(4):
        for g in range(8):
            o_ref[40 * a2 + 5 * g : 40 * a2 + 5 * g + 5, :] = o_s[a2, g, 0:5, :]


def place(scal, chunks, arrays):
    full = pl.BlockSpec(memory_space=pltpu.VMEM)
    return pl.pallas_call(
        functools.partial(place_kernel, chunks),
        out_shape=jax.ShapeDtypeStruct((160, 800), jnp.float32),
        in_specs=[pl.BlockSpec(memory_space=pltpu.SMEM)] + [full] * len(arrays),
        out_specs=full,
        scratch_shapes=[pltpu.VMEM((4, 8, 8, 800), jnp.float32)],
        compiler_params=pltpu.CompilerParams(vmem_limit_bytes=VLIM),
        cost_estimate=pl.CostEstimate(flops=1_000_000, bytes_accessed=3_000_000, transcendentals=0),
        name="place",
    )(scal, *arrays)


def cidx(z, y, x):
    return (z % 4) * 8 + (y % 2) * 4 + x % 4


def shift(dz=0, dy=0, dx=0):
    return [(cidx(z, y, x), cidx(z + dz, y + dy, x + dx)) for z in range(4) for y in range(2) for x in range(4)]


XP, XM, ZP, ZM, YY = shift(dx=1), shift(dx=-1), shift(dz=1), shift(dz=-1), shift(dy=1)
X2, Z2 = shift(dx=2), shift(dz=2)


def send(v, perm):
    return lax.ppermute(v, "col", perm)


def after(v, *others):
    return lax.optimization_barrier((v, *others))[0]


def to_core(outs):
    return lax.ppermute(outs[2], "row", [(r, r ^ 1) for r in range(4)])


def to_partner(outs, got):
    rows = outs[1].shape[0]
    return lax.ppermute(outs[1] + got[rows:], "row", [(r, r ^ 2) for r in range(4)])


def per_device(pair_amps, cycle_w):
    c, r = lax.axis_index("col"), lax.axis_index("row")
    x0, y0, z0 = c % 4, (c // 4) % 2, c // 8
    scal = jnp.stack([c % 2, x0, r, z0, y0]).astype(jnp.int32)
    wt = cycle_w.T
    pay0, pay1 = pack(scal, pair_amps)
    pay0, pay1 = pay0.reshape(1, PAY, 8, 128), pay1.reshape(1, PAY, 8, 128)

    f0, f1 = send(pay0, X2), send(pay1, Z2)
    near0, near1 = join((pay0, pay1), (0,), (1,))
    m0, m1 = send(near0, XP), send(near1, ZP)
    p0, p1 = send(near0, XM), send(near1, ZM)
    g0, g1 = join((pay0, m0, p0, f0, pay1, m1, p1, f1), (0, 1, 2, 3), (4, 5, 6, 7))

    zm, zp = send(g0, ZP), send(g0, ZM)
    xm, xp = send(g1, XP), send(g1, XM)
    y0g = send(g0, YY)
    *w, tok_b = split_weights(after(wt, g0))
    zm, zp, xm, xp, y0g = (after(v, tok_b) for v in (zm, zp, xm, xp, y0g))
    zf, zb = send(zm[:2], ZP), send(zp[2:], ZM)
    xf, xb = send(xm[:2], XP), send(xp[2:], XM)
    y1g = send(after(g1, y0g), YY)

    yzm, yzp = send(after(y0g, zf), ZP), send(after(y0g, zb), ZM)
    yxm, yxp = send(after(y1g, xf), XP), send(after(y1g, xb), XM)

    every = lambda own: range(5)
    early = functools.partial(lines_at, late=False)
    late = functools.partial(lines_at, late=True)
    whole = lambda op: (lambda own, x: (op, (0, 2, 3, 1)[(x - own) % 4]), every)
    halves = lambda lo, hi: (lambda own, x: ((lo, 0), (hi, 0), (hi, 1), (lo, 1))[(x - own) % 4], every)
    ring = lambda s, of, lines: (lambda own, x: of[(x - own) % 4](s), lines)
    plus = lambda dz: lambda z: lax.rem(z + dz, 4)
    column = (0, 3, 1, 2)
    of = [lambda s: (6, s), lambda s: (8, s), lambda s: (9 + s // 2, s % 2), lambda s: (7, s)]
    oa = product(
        scal,
        [g0, zm, zp, zf, zb, y0g, g1, xm, xp, xf, xb],
        [whole(0), whole(1), whole(2), halves(3, 4), whole(5)] + [ring(s, of, every) for s in range(4)],
        w,
    )
    sa = [(0, plus(d), 0, every) for d in column] + [(0, plus(0), 1, every)] + [(1, plus(d), 0, every) for d in column]
    yzm, yzp, yxm, yxp = (after(v, oa[0]) for v in (yzm, yzp, yxm, yxp))
    yxf, yxb = send(yxm[:2], XP), send(yxp[2:], XM)
    yzf, yzb = send(yzm[:2], ZP), send(yzp[2:], ZM)
    got_a = to_core(oa)
    of = [lambda s: (2, s), lambda s: (4, s), None, lambda s: (3, s)]
    ob = product(
        scal,
        [after(yzm, got_a), yzp, y1g, yxm, yxp],
        [whole(0), whole(1)] + [ring(s, of, early) for s in range(4)],
        w,
    )
    sb = [(0, plus(3), 1, every), (0, plus(1), 1, every)] + [(1, plus(d), 1, early) for d in column]
    sums_a = [oa[0], got_a, to_partner(oa, got_a)]
    yzf = after(yzf, ob[0], sums_a[2])
    of = [lambda s: (2, s), lambda s: (4, s), lambda s: (5 + s // 2, s % 2), lambda s: (3, s)]
    oc = product(
        scal,
        [yzf, yzb, y1g, yxm, yxp, yxf, yxb],
        [halves(0, 1)] + [ring(s, of, late) for s in range(4)],
        w,
        ob,
    )
    sc = [(0, plus(2), 1, every)] + [(1, plus(d), 1, late) for d in column]
    got_c = to_core(oc)
    sums_c = [oc[0], got_c, to_partner(oc, got_c)]
    return place(scal, ((sa,), (sb, sc)), sums_a + sums_c)


def solution(mesh):
    return jax.shard_map(
        per_device,
        mesh=mesh,
        in_specs=(P("row", "col"), P("row", "col")),
        out_specs=P("row", "col"),
        check_vma=False,
    )
```

```python
import functools

import jax
import jax.numpy as jnp
from jax import lax
from jax.experimental import pallas as pl
from jax.experimental.pallas import tpu as pltpu
from jax.sharding import PartitionSpec as P

O = 40
PAY = 63
KMAIN, KTAIL = 5120, 1280
KBLK = 1280
VLIM = 16 * 1024 * 1024
SPLIT_VLIM = 28 * 1024 * 1024
ORDER = (6, 0, 1, 2, 3, 4, 5)


def pack_kernel(sc_ref, p_ref, o0_ref, o1_ref, main, tail):
    base = pl.multiple_of(sc_ref[0] * 32, 32)
    tail[...] = jnp.zeros_like(tail)
    for k in range(7):
        if k < 6:
            x = p_ref[:, 128 * k : 128 * k + 128]
            rows = 128
        else:
            x = jnp.concatenate([p_ref[:, 768:800], jnp.zeros((160, 96), jnp.float32)], axis=1)
            rows = 32
        x = jnp.concatenate([x, jnp.zeros((96, 128), jnp.float32)], axis=0)
        xt = x.T
        main[128 * k : 128 * k + rows, :] = xt[:rows, :128]
        tail[pl.ds(base + 128 * k, rows), :] = xt[:rows, 128:]
    for h, o_ref in ((0, o0_ref), (1, o1_ref)):
        for s in range(8):
            a = 4 * (s // 2) + 2 * h + s % 2
            o_ref[pl.ds(s, 50, stride=8), :] = main[pl.ds(a, 50, stride=16), :]
            t = tail[pl.ds(a, 13, stride=64), :]
            for q in range(1, 4):
                t = t + pltpu.roll(tail[pl.ds(16 * q + a, 13, stride=64), :], 32 * q, 1)
            o_ref[pl.ds(400 + s, 13, stride=8), :] = t


def pack(scal, p):
    full = pl.BlockSpec(memory_space=pltpu.VMEM)
    return pl.pallas_call(
        pack_kernel,
        out_shape=[jax.ShapeDtypeStruct((PAY * 8, 128), jnp.float32)] * 2,
        in_specs=[pl.BlockSpec(memory_space=pltpu.SMEM), full],
        out_specs=[full, full],
        scratch_shapes=[pltpu.VMEM((800, 128), jnp.float32), pltpu.VMEM((832, 128), jnp.float32)],
        compiler_params=pltpu.CompilerParams(vmem_limit_bytes=VLIM),
        cost_estimate=pl.CostEstimate(flops=0, bytes_accessed=1_000_000, transcendentals=0),
        name="pack",
    )(scal, p)


def join_kernel(lists, *refs):
    ins, outs = refs[: -len(lists)], refs[-len(lists) :]
    for out, which in zip(outs, lists):
        at = 0
        for k in which:
            out[at : at + ins[k].shape[0]] = ins[k][...]
            at += ins[k].shape[0]


def join(arrays, *lists):
    vmem = pl.BlockSpec(memory_space=pltpu.VMEM)
    return pl.pallas_call(
        functools.partial(join_kernel, lists),
        out_shape=[
            jax.ShapeDtypeStruct((sum(arrays[k].shape[0] for k in which), PAY, 8, 128), jnp.float32) for which in lists
        ],
        in_specs=[vmem] * len(arrays),
        out_specs=[vmem] * len(lists),
        compiler_params=pltpu.CompilerParams(vmem_limit_bytes=VLIM),
        cost_estimate=pl.CostEstimate(flops=0, bytes_accessed=1_000_000, transcendentals=0),
        name="join",
    )(*arrays)


NA, NB = 256, 512
WIDE_A, WIDE_B = 2 * NA, 2 * NB + 128


def split_kernel(wt_ref, a_ref, b_ref, tok_ref, buf, tr, sem):
    def fetch(at):
        n = ORDER[at]
        rows = 128 if n < 6 else 32
        return pltpu.make_async_copy(wt_ref.at[pl.ds(128 * n, rows)], buf.at[at % 2, pl.ds(0, rows)], sem.at[at % 2])

    def turn(at, kt):
        k = pl.ds(pl.multiple_of(kt * 128, 128), 128)
        if ORDER[at] < 6:
            tr[at % 2, k, :] = buf[at % 2, :, k].T
        else:
            tr[at % 2, k, 0:32] = buf[at % 2, 0:32, k].T

    def store(at, j):
        n = ORDER[at]
        o_ref = a_ref if n < 2 else b_ref
        hi_at = 128 * n if n < 2 else 128 * (n - 2)
        lo_at = hi_at + (NA if n < 2 else NB + 128)
        x = tr[at % 2, pl.ds(j, 160, stride=O), :]
        if n == 6:
            lane = lax.broadcasted_iota(jnp.int32, x.shape, 1)
            x = jnp.where(lane < 32, x, 0.0)
        hi = x.astype(jnp.bfloat16)
        res = x - hi.astype(jnp.float32)
        m = pl.ds(pl.multiple_of(j * 128, 128), 128)
        t = pl.ds(pl.multiple_of(KMAIN + j * 32, 32), 32)
        if n == 6:
            hi = (hi.astype(jnp.float32) + pltpu.roll(res, 32, 1)).astype(jnp.bfloat16)
        o_ref[m, hi_at : hi_at + 128] = hi[:128]
        o_ref[t, hi_at : hi_at + 128] = hi[128:]
        if n < 6:
            lo = res.astype(jnp.bfloat16)
            o_ref[m, lo_at : lo_at + 128] = lo[:128]
            o_ref[t, lo_at : lo_at + 128] = lo[128:]

    count = len(ORDER)
    fetch(0).start()
    for at in range(count + 1):
        if at + 1 < count:
            fetch(at + 1).start()
        if at < count:
            fetch(at).wait()

        @pl.loop(0, 5)
        def _(u):
            if at < count:
                for v in range(10):
                    turn(at, 10 * u + v)
            if at > 0:
                for v in range(8):
                    store(at - 1, 8 * u + v)

    tok_ref[...] = jnp.zeros_like(tok_ref)


def split_weights(wt):
    vmem = pl.BlockSpec(memory_space=pltpu.VMEM)
    return pl.pallas_call(
        split_kernel,
        out_shape=[
            jax.ShapeDtypeStruct((6400, WIDE_A), jnp.bfloat16),
            jax.ShapeDtypeStruct((6400, WIDE_B), jnp.bfloat16),
            jax.ShapeDtypeStruct((8, 128), jnp.float32),
        ],
        in_specs=[pl.BlockSpec(memory_space=pltpu.HBM)],
        out_specs=[vmem, vmem, vmem],
        scratch_shapes=[
            pltpu.VMEM((2, 128, 6400), jnp.float32),
            pltpu.VMEM((2, 6400, 128), jnp.float32),
            pltpu.SemaphoreType.DMA((2,)),
        ],
        compiler_params=pltpu.CompilerParams(vmem_limit_bytes=SPLIT_VLIM),
        cost_estimate=pl.CostEstimate(flops=0, bytes_accessed=45_000_000, transcendentals=0),
        name="split_w",
    )(wt)


def lines_at(own, late):
    first = 5 * ((own + 2) % 4) // 4
    return [first, first + 1] if late else [(first + k) % 5 for k in (2, 3, 4)]


def product_kernel(places, carried, sc_ref, *refs):
    n_in = len(refs) - 11 - (3 if carried else 0)
    ins, (wa, wb) = refs[:n_in], refs[n_in : n_in + 2]
    before, outs = refs[n_in + 2 : -9], refs[-9:-6]
    lhs, acc1, acc2, zs, main, tail = refs[-6:]
    x0, r0 = sc_ref[1], sc_ref[2]
    slots = len(places)
    n5 = sum(len(lines(0)) for _, lines in places)
    rows = 8 * n5
    mp = lhs.shape[0] // 2

    def put(at, parts):
        v = jnp.concatenate(parts, axis=0)
        if mp > rows:
            v = jnp.concatenate([v, jnp.zeros((mp - rows, 128), jnp.float32)], axis=0)
        hi = v.astype(jnp.bfloat16)
        lhs[0:mp, at * 128 : at * 128 + 128] = hi
        lhs[mp:, at * 128 : at * 128 + 128] = (v - hi.astype(jnp.float32)).astype(jnp.bfloat16)

    tail[...] = jnp.zeros_like(tail)
    for s, (where, _) in enumerate(places):
        for d in range(4):
            if where(0, d) is None:
                continue
            op, at = where(0, d)
            x = lax.rem(x0 + d, 4)
            main[s, pl.ds(50 * x, 50)] = ins[op][at, 0:50]
            tail[s, pl.ds(25 * (x // 2) + 12 * lax.rem(x, 2), 13)] += ins[op][at, 50:63]

    chosen = [lines(x0) for _, lines in places]

    def fill(kb):
        for jj in range(10):
            if kb < 4:
                put(jj, [main[s, 40 * i + 10 * kb + jj] for s, lines in enumerate(chosen) for i in lines])
            else:
                put(jj, [tail[s, 10 * i + jj] for s, lines in enumerate(chosen) for i in lines])

    dot = functools.partial(jnp.dot, preferred_element_type=jnp.float32)
    for kb in range(5):
        fill(kb)
        k = slice(kb * KBLK, kb * KBLK + KBLK)
        one = dot(lhs[...], wa[k, 0:NA]), dot(lhs[...], wb[k, 0 : NB + 128])
        two = dot(lhs[0:mp], wa[k, NA:]), dot(lhs[0:mp], wb[k, NB + 128 :])
        if kb == 0:
            acc1[:, 0:NA], acc1[:, NA:] = one
            acc2[:, 0:NA], acc2[:, NA:] = two
        else:
            acc1[:, 0:NA] += one[0]
            acc1[:, NA:] += one[1]
            acc2[:, 0:NA] += two[0]
            acc2[:, NA:] += two[1]

    for n in range(7):
        lanes = slice(128 * n, 128 * n + 128)
        z = acc1[0:rows, lanes] + acc1[mp : mp + rows, lanes]
        if n < 6:
            z = z + acc2[0:rows, lanes]
        else:
            z = z + pltpu.roll(acc1[0:rows, lanes], 96, 1)
        zs[n] = z
    for out, at, k in ((0, 0, 0), (1, 0, 2), (2, 0, 1), (2, carried + 2 * n5, 3)):
        to = jnp.bitwise_xor(r0, k)
        if carried:
            have = slice(carried, 2 * carried) if k == 3 else slice(0, carried)
            outs[out][at : at + carried, :] = before[out][have, :]
            at += carried
        for e in range(2):
            for n in range(7):
                wide = 128 if n < 6 else 32
                v = zs[n, pl.ds(2 * to + e, n5, stride=8), :]
                outs[out][at + e * n5 : at + e * n5 + n5, 128 * n : 128 * n + wide] = v[:, :wide]


def product(scal, operands, places, w, before=()):
    n5 = sum(len(lines(0)) for _, lines in places)
    carried = before[0].shape[0] if before else 0
    mp = -(-8 * n5 // 16) * 16
    f32, bf16 = jnp.float32, jnp.bfloat16
    vmem = pl.BlockSpec(memory_space=pltpu.VMEM)
    return pl.pallas_call(
        functools.partial(product_kernel, places, carried),
        out_shape=[jax.ShapeDtypeStruct((k * (carried + 2 * n5), 800), f32) for k in (1, 1, 2)],
        in_specs=[pl.BlockSpec(memory_space=pltpu.SMEM)] + [vmem] * (len(operands) + 2 + len(before)),
        out_specs=[vmem] * 3,
        scratch_shapes=[
            pltpu.VMEM((2 * mp, KBLK), bf16),
            pltpu.VMEM((2 * mp, 896), f32),
            pltpu.VMEM((mp, 768), f32),
            pltpu.VMEM((7, 8 * n5, 128), f32),
            pltpu.VMEM((len(places), 200, 8, 128), f32),
            pltpu.VMEM((len(places), 50, 8, 128), f32),
        ],
        compiler_params=pltpu.CompilerParams(vmem_limit_bytes=VLIM),
        cost_estimate=pl.CostEstimate(flops=8 * n5 * 6400 * 800 * 6, bytes_accessed=22_000_000, transcendentals=0),
        name="product",
    )(scal, *operands, *w, *before)


def place_kernel(chunks, sc_ref, *refs):
    o_ref, o_s = refs[-2], refs[-1]
    x0, z0, y0 = sc_ref[1], sc_ref[3], sc_ref[4]

    def put(v, at_x, parts):
        at = 0
        for slots in parts:
            for half_e in range(2):
                for h, z_of, dy, lines in slots:
                    g = 2 * z_of(z0) + lax.rem(y0 + dy, 2)
                    for i in lines(at_x):
                        o_s[2 * h + half_e, g, i : i + 1, :] = v[at : at + 1, :]
                        at += 1

    for c, parts in enumerate(chunks):
        mine, core, across = refs[3 * c : 3 * c + 3]
        v = mine[...] + core[0 : mine.shape[0]] + across[...]
        for at_x in range(4):
            pl.when(x0 == at_x)(functools.partial(put, v, at_x, parts))
    for a2 in range(4):
        for g in range(8):
            o_ref[40 * a2 + 5 * g : 40 * a2 + 5 * g + 5, :] = o_s[a2, g, 0:5, :]


def place(scal, chunks, arrays):
    full = pl.BlockSpec(memory_space=pltpu.VMEM)
    return pl.pallas_call(
        functools.partial(place_kernel, chunks),
        out_shape=jax.ShapeDtypeStruct((160, 800), jnp.float32),
        in_specs=[pl.BlockSpec(memory_space=pltpu.SMEM)] + [full] * len(arrays),
        out_specs=full,
        scratch_shapes=[pltpu.VMEM((4, 8, 8, 800), jnp.float32)],
        compiler_params=pltpu.CompilerParams(vmem_limit_bytes=VLIM),
        cost_estimate=pl.CostEstimate(flops=1_000_000, bytes_accessed=3_000_000, transcendentals=0),
        name="place",
    )(scal, *arrays)


def cidx(z, y, x):
    return (z % 4) * 8 + (y % 2) * 4 + x % 4


def shift(dz=0, dy=0, dx=0):
    return [(cidx(z, y, x), cidx(z + dz, y + dy, x + dx)) for z in range(4) for y in range(2) for x in range(4)]


XP, XM, ZP, ZM, YY = shift(dx=1), shift(dx=-1), shift(dz=1), shift(dz=-1), shift(dy=1)
X2, Z2 = shift(dx=2), shift(dz=2)


def send(v, perm):
    return lax.ppermute(v, "col", perm)


def after(v, *others):
    return lax.optimization_barrier((v, *others))[0]


def to_core(outs):
    return lax.ppermute(outs[2], "row", [(r, r ^ 1) for r in range(4)])


def to_partner(outs, got):
    rows = outs[1].shape[0]
    return lax.ppermute(outs[1] + got[rows:], "row", [(r, r ^ 2) for r in range(4)])


def per_device(pair_amps, cycle_w):
    c, r = lax.axis_index("col"), lax.axis_index("row")
    x0, y0, z0 = c % 4, (c // 4) % 2, c // 8
    scal = jnp.stack([c % 2, x0, r, z0, y0]).astype(jnp.int32)
    wt = cycle_w.T
    pay0, pay1 = pack(scal, pair_amps)
    pay0, pay1 = pay0.reshape(1, PAY, 8, 128), pay1.reshape(1, PAY, 8, 128)

    f0, f1 = send(pay0, X2), send(pay1, Z2)
    near0, near1 = join((pay0, pay1), (0,), (1,))
    m0, m1 = send(near0, XP), send(near1, ZP)
    p0, p1 = send(near0, XM), send(near1, ZM)
    g0, g1 = join((pay0, m0, p0, f0, pay1, m1, p1, f1), (0, 1, 2, 3), (4, 5, 6, 7))

    zm, zp = send(g0, ZP), send(g0, ZM)
    xm, xp = send(g1, XP), send(g1, XM)
    y0g = send(g0, YY)
    *w, tok_b = split_weights(after(wt, g0))
    zm, zp, xm, xp, y0g = (after(v, tok_b) for v in (zm, zp, xm, xp, y0g))
    zf, zb = send(zm[:2], ZP), send(zp[2:], ZM)
    xf, xb = send(xm[:2], XP), send(xp[2:], XM)
    y1g = send(after(g1, y0g), YY)

    yzm, yzp = send(after(y0g, zf), ZP), send(after(y0g, zb), ZM)
    yxm, yxp = send(after(y1g, xf), XP), send(after(y1g, xb), XM)

    every = lambda own: range(5)
    early = functools.partial(lines_at, late=False)
    late = functools.partial(lines_at, late=True)
    whole = lambda op: (lambda own, x: (op, (0, 2, 3, 1)[(x - own) % 4]), every)
    halves = lambda lo, hi: (lambda own, x: ((lo, 0), (hi, 0), (hi, 1), (lo, 1))[(x - own) % 4], every)
    ring = lambda s, of, lines: (lambda own, x: of[(x - own) % 4] and of[(x - own) % 4](s), lines)
    plus = lambda dz: lambda z: lax.rem(z + dz, 4)
    column = (0, 3, 1, 2)
    of = [lambda s: (6, s), lambda s: (8, s), lambda s: (9 + s // 2, s % 2), lambda s: (7, s)]
    oa = product(
        scal,
        [g0, zm, zp, zf, zb, y0g, g1, xm, xp, xf, xb],
        [whole(0), whole(1), whole(2), halves(3, 4), whole(5)] + [ring(s, of, every) for s in range(4)],
        w,
    )
    sa = [(0, plus(d), 0, every) for d in column] + [(0, plus(0), 1, every)] + [(1, plus(d), 0, every) for d in column]
    yzm, yzp, yxm, yxp = (after(v, oa[0]) for v in (yzm, yzp, yxm, yxp))
    yxf, yxb = send(yxm[:2], XP), send(yxp[2:], XM)
    yzf, yzb = send(yzm[:2], ZP), send(yzp[2:], ZM)
    got_a = to_core(oa)
    of = [lambda s: (2, s), lambda s: (4, s), None, lambda s: (3, s)]
    ob = product(
        scal,
        [after(yzm, got_a), yzp, y1g, yxm, yxp],
        [whole(0), whole(1)] + [ring(s, of, early) for s in range(4)],
        w,
    )
    sb = [(0, plus(3), 1, every), (0, plus(1), 1, every)] + [(1, plus(d), 1, early) for d in column]
    sums_a = [oa[0], got_a, to_partner(oa, got_a)]
    yzf = after(yzf, ob[0], sums_a[2])
    of = [lambda s: (2, s), lambda s: (4, s), lambda s: (5 + s // 2, s % 2), lambda s: (3, s)]
    oc = product(
        scal,
        [yzf, yzb, y1g, yxm, yxp, yxf, yxb],
        [halves(0, 1)] + [ring(s, of, late) for s in range(4)],
        w,
        ob,
    )
    sc = [(0, plus(2), 1, every)] + [(1, plus(d), 1, late) for d in column]
    got_c = to_core(oc)
    sums_c = [oc[0], got_c, to_partner(oc, got_c)]
    return place(scal, ((sa,), (sb, sc)), sums_a + sums_c)


def solution(mesh):
    return jax.shard_map(
        per_device,
        mesh=mesh,
        in_specs=(P("row", "col"), P("row", "col")),
        out_specs=P("row", "col"),
        check_vma=False,
    )
```
